1024 devices in a mesh: user: 64 (over x, y_hi, core), item: 16 (over y_lo, z).
Axes of the slice: x: 8, y: 8 (y_hi: 4, y_lo: 2; y = y_hi * 2 + y_lo), z: 8, core: 2. Of those that a mesh axis runs over, the one named last changes fastest.
Arguments:
- users: float32 [65536, 256], P(('user', 'item')), may hold values from -1.5 to 1.5
- user_accum: float32 [65536, 256], P(('user', 'item')), may hold values from 0.1 to 10
- items: float32 [262144, 256], P(('user', 'item')), may hold values from -1.5 to 1.5
- item_accum: float32 [262144, 256], P(('user', 'item')), may hold values from 0.1 to 10
- ratings: int32 [2, 65536, 4096], P(None, 'user', 'item'), may hold values from 0 to 1
- tile_mask: int32 [2, 512, 32], P(None, 'user', 'item'), may hold values 0 or 1
Outputs:
- users_out: float32 [65536, 256], P(('user', 'item'))
- items_out: float32 [262144, 256], P(('user', 'item'))
The draws below stay inside these ranges and needn't reach their ends.
All inputs are finite; a program needn't handle non-finite values. No bound on the sum of `tile_mask` on one device may be relied on, other than what follows from the above.
Results may differ from the reference program's by a relative error of at most 0.013.
Values may be sent and summed in bfloat16 or wider, within the bound.
A program may use at most 32 MiB of HBM per device.

```python
import math
import jax
import jax.numpy as jnp
from jax import lax

R = 256
TILE = 128
STRATA = 2
USERS = 65536
BLK = 4096
ITEMS = 262144
N_USER = 64


def touch_ends(values, stream_key, least, top_value):
    place = [jax.random.randint(jax.random.fold_in(stream_key, axis), (), 0, length) for axis, length in enumerate(values.shape)]
    widest = values.shape.index(max(values.shape))
    neighbour = place[:widest] + [(place[widest] + 1) % values.shape[widest]] + place[widest + 1:]
    return values.at[tuple(place)].set(least).at[tuple(neighbour)].set(top_value)


def shard_levels(stream_key, dims, cuts, least, largest):
    def one(dim, shards_of):
        draws = jax.random.uniform(jax.random.fold_in(jax.random.fold_in(stream_key, 6), dim), (shards_of,), jnp.float32, least / len(cuts), largest / len(cuts))
        return jnp.repeat(jnp.exp(draws), dims[dim] // shards_of).reshape((-1,) + (1,) * (len(dims) - dim - 1))

    gain = one(*cuts[0])
    for cut in cuts[1:]:
        gain = gain * one(*cut)
    return gain


def bell_draw(rng, shape, deviation, reach, split=(), kind=jnp.bfloat16):
    array = jax.random.normal(rng, shape, jnp.float32) * deviation
    if len(split) > 0:
        array = shard_levels(rng, shape, split, -0.22, 0.18) * array
    return jnp.clip(array, min=-reach, max=reach).astype(kind)


def setup_inputs(seed: int = 0) -> dict:
    key_list = jax.random.split(jax.random.key(seed), 7)
    return {
        "users": bell_draw(key_list[0], (USERS, R), 0.25, 1.5, ((0, 1024),), jnp.float32),
        "user_accum": jnp.clip(jnp.exp(math.log(10.0) - 4.6051702 * jax.random.uniform(key_list[1], (USERS, R), jnp.float32) ** shard_levels(key_list[1], (USERS, R), ((0, 1024),), -0.2, 0.2)), 0.1, 10.0),
        "items": bell_draw(key_list[2], (ITEMS, R), 0.25, 1.5, ((0, 1024),), jnp.float32),
        "item_accum": jnp.clip(jnp.exp(math.log(10.0) - 4.6051702 * jax.random.uniform(key_list[3], (ITEMS, R), jnp.float32) ** shard_levels(key_list[3], (ITEMS, R), ((0, 1024),), -0.2, 0.2)), 0.1, 10.0),
        "ratings": touch_ends(jax.random.randint(key_list[4], (STRATA, USERS, BLK), 0, 2), jax.random.fold_in(key_list[4], 1), 0, 1).astype(jnp.int32),
        "tile_mask": touch_ends((jax.random.randint(key_list[5], (STRATA, USERS // TILE, BLK // TILE), 0, 5) < 3).astype(jnp.int32), jax.random.fold_in(key_list[5], 1), 0, 1),
    }


def adagrad(param, accum, grad):
    accum = accum + grad * grad
    return (param - 0.25 * grad / (jnp.sqrt(accum) + 1e-06), accum)

def expand_mask(mask, rows, cols):
    full = jnp.broadcast_to(mask.astype(jnp.float32)[:, None, :, None], (rows // TILE, TILE, cols // TILE, TILE))
    return full.reshape(rows, cols)

def one_block(packed):
    user_rows, user_acc, item_rows, item_acc, rates, mask = packed
    user_bf = user_rows.astype(jnp.bfloat16)
    item_bf = item_rows.astype(jnp.bfloat16)
    logits = lax.dot_general(user_bf, item_bf, (((1,), (1,)), ((), ())), preferred_element_type=jnp.float32)
    observed = expand_mask(mask, user_rows.shape[0], item_rows.shape[0])
    errors = (observed * (jax.nn.sigmoid(logits) - rates.astype(jnp.float32))).astype(jnp.bfloat16)
    user_grad = jnp.dot(errors, item_bf, preferred_element_type=jnp.float32) + 0.1 * user_rows
    item_grad = lax.dot_general(errors, user_bf, (((0,), (0,)), ((), ())), preferred_element_type=jnp.float32) + 0.1 * item_rows
    new_users, new_uacc = adagrad(user_rows, user_acc, user_grad)
    new_items, new_iacc = adagrad(item_rows, item_acc, item_grad)
    return (new_users, new_uacc, new_items, new_iacc)

def reference(users, user_accum, items, item_accum, ratings, tile_mask):
    block_users = users.shape[0] // N_USER
    block_items = items.shape[0] // N_USER
    rank = users.shape[1]
    for stratum in range(STRATA):
        ublocks = users.reshape(N_USER, block_users, rank)
        uacc = user_accum.reshape(N_USER, block_users, rank)
        iblocks = jnp.roll(items.reshape(N_USER, block_items, rank), stratum, axis=0)
        iacc = jnp.roll(item_accum.reshape(N_USER, block_items, rank), stratum, axis=0)
        rates = ratings[stratum].reshape(N_USER, block_users, block_items)
        masks = tile_mask[stratum].reshape(N_USER, block_users // TILE, block_items // TILE)
        new_u, new_ua, new_i, new_ia = lax.map(one_block, (ublocks, uacc, iblocks, iacc, rates, masks))
        users = new_u.reshape(-1, rank)
        user_accum = new_ua.reshape(-1, rank)
        items = jnp.roll(new_i, -stratum, axis=0).reshape(-1, rank)
        item_accum = jnp.roll(new_ia, -stratum, axis=0).reshape(-1, rank)
    return (users, items)
```

```python
import functools
import math

import jax
import jax.numpy as jnp
from jax import lax
from jax.experimental import pallas as pl
from jax.experimental.pallas import tpu as pltpu
from jax.sharding import PartitionSpec as P

MESH = pl.DeviceIdType.MESH
RING = 8

NODES = (
    (0, 0, None),
    (0, 2, 0),
    (0, -2, 0),
    (1, 0, 0),
    (0, 1, 0),
    (0, -1, 0),
    (0, 4, 1),
    (1, 2, 1),
    (0, 3, 1),
    (1, -2, 2),
    (0, -3, 2),
    (1, 1, 3),
    (1, -1, 3),
    (1, 4, 6),
    (1, 3, 7),
    (1, -3, 9),
)
GROUPS = ((0, 6), (6, 13), (13, 16))


FLOOR, TOP = 1 / 16, 8192.0
STEPS = 32767 / math.log(1 + TOP / FLOOR)


def encode(x):
    steps = jnp.minimum(STEPS * jnp.log(1.0 + jnp.abs(x) * (1 / FLOOR)) + 0.5, 32767.0)
    return jnp.where(x < 0, -steps, steps).astype(jnp.int32).astype(jnp.int16)


def decode(code):
    steps = code.astype(jnp.int32).astype(jnp.float32)
    size = FLOOR * jnp.exp(jnp.abs(steps) * (1 / STEPS)) - FLOOR
    return jnp.where(steps < 0, -size, size)


def children_of(node):
    return [n for n, row in enumerate(NODES) if row[2] == node]


def hop(start, end):
    return (NODES[end][0] - NODES[start][0]) % 2, NODES[end][1] - NODES[start][1]


def peers():
    found = set()
    for node, row in enumerate(NODES):
        if row[2] is not None:
            dy, dz = hop(row[2], node)
            found |= {(dy, dz % RING), (dy, -dz % RING)}
    return sorted(found)


def adagrad(param, accum, grad):
    accum = accum + grad * grad
    return param - 0.25 * grad / (jnp.sqrt(accum) + 1e-06), accum


def kernel(
    n_user, users_h, uacc_h, items_h, iacc_h, rates_h, mask_h, users_o, items_o,
    rates, mask, user_v, uacc_v, item_v, iacc_v, item_b, gather, errors, parts, outgo, income, grad_out, grad_in,
    load_sem, gs_send, gs_recv, rs_send, rs_recv, it_send, it_recv,
):
    f32, bf16 = jnp.float32, jnp.bfloat16
    strata = rates_h.shape[0]
    rows = users_h.shape[0]
    cols = items_h.shape[0]
    tile_rows = len(NODES) * rows // mask_h.shape[2]
    tile_cols = cols // mask_h.shape[1]
    u, i = lax.axis_index("user"), lax.axis_index("item")
    y, z = i // RING, i % RING
    after, before = (u + 1) % n_user, (u + n_user - 1) % n_user

    loads = [
        (users_h, user_v), (items_h, item_v), (mask_h, mask), (rates_h.at[0], rates.at[0]),
        (iacc_h, iacc_v), (uacc_h, uacc_v), (rates_h.at[1], rates.at[1]),
    ]
    loads = [pltpu.make_async_copy(src, dst, load_sem.at[k]) for k, (src, dst) in enumerate(loads)]
    for load in loads:
        load.start()

    barrier = pltpu.get_barrier_semaphore()
    near = peers()
    for dy, dz in near:
        there = (u, ((y + dy) % 2) * RING + (z + dz) % RING)
        pl.semaphore_signal(barrier, inc=1, device_id=there, device_id_type=MESH)
    for v in (after, before):
        pl.semaphore_signal(barrier, inc=1, device_id=(v, i), device_id_type=MESH)

    def side(node):
        return 1 - 2 * ((z + NODES[node][1] + RING) % 2)

    def owner(node):
        dy, dz, _ = NODES[node]
        return ((y + dy) % 2) * RING + (z - side(node) * dz + RING) % RING

    def target(start, end):
        dy, dz = hop(start, end)
        return (u, ((y + dy) % 2) * RING + (z + side(start) * dz + RING) % RING)

    def block(node):
        return pl.ds(node * rows, rows)

    def down(s, node, child):
        return pltpu.make_async_remote_copy(
            src_ref=gather.at[s, block(node)], dst_ref=gather.at[s, block(child)],
            send_sem=gs_send.at[s, child], recv_sem=gs_recv.at[s, child],
            device_id=target(node, child), device_id_type=MESH,
        )

    def up(s, node):
        return pltpu.make_async_remote_copy(
            src_ref=outgo.at[s, block(node)], dst_ref=income.at[s, block(node)],
            send_sem=rs_send.at[s, node], recv_sem=rs_recv.at[s, node],
            device_id=target(node, NODES[node][2]), device_id_type=MESH,
        )

    items_on = pltpu.make_async_remote_copy(
        src_ref=item_b.at[2], dst_ref=item_b.at[1], send_sem=it_send.at[0], recv_sem=it_recv.at[0],
        device_id=(after, i), device_id_type=MESH,
    )
    grads_back = pltpu.make_async_remote_copy(
        src_ref=grad_out, dst_ref=grad_in, send_sem=it_send.at[1], recv_sem=it_recv.at[1],
        device_id=(before, i), device_id_type=MESH,
    )

    def compute(s, first, last):
        item_rows = item_b[s]
        span = slice(first * rows, last * rows)
        logits = lax.dot_general(
            gather[s, span, :], item_rows, (((1,), (1,)), ((), ())), preferred_element_type=f32
        )
        half = 0.5 * jnp.tanh(0.5 * logits) + 0.5
        for node in range(first, last):
            own = owner(node)
            at = pl.ds(pl.multiple_of(own * rows, rows), rows)
            mine = half[(node - first) * rows : (node - first + 1) * rows]
            wrong = mine - rates[s, at, :].astype(f32)
            for t in range(cols // tile_cols):
                seen = mask[s, t, own * rows // tile_rows].astype(f32)
                c = slice(t * tile_cols, (t + 1) * tile_cols)
                errors[block(node), c] = (seen * wrong[:, c]).astype(bf16)
        share = jnp.dot(errors[span, :], item_rows, preferred_element_type=f32)
        for node in range(first, last):
            mine = share[(node - first) * rows : (node - first + 1) * rows]
            if node > 0 and not children_of(node):
                outgo[s, block(node), :] = encode(mine)
                up(s, node).start()
            else:
                parts[block(node), :] = mine

    loads[0].wait()
    gather[0, block(0), :] = user_v[...].astype(bf16)
    pl.semaphore_wait(barrier, len(near) + 2)

    for s in range(strata):
        for child in children_of(0):
            down(s, 0, child).start()
        if s == 0:
            loads[1].wait()
            item_b[0] = item_v[...].astype(bf16)
            loads[2].wait()
            loads[3].wait()
        else:
            loads[6].wait()
            items_on.wait_recv()
        for first, last in GROUPS:
            for node in range(max(first, 1), last):
                down(s, NODES[node][2], node).wait_recv()
                for child in children_of(node):
                    down(s, node, child).start()
            compute(s, first, last)

        item_grad = lax.dot_general(
            errors[...], gather[s], (((0,), (0,)), ((), ())), preferred_element_type=f32
        )
        if s == 0:
            loads[4].wait()
            new_items, new_iacc = adagrad(item_v[...], iacc_v[...], item_grad + 0.1 * item_v[...])
            item_v[...] = new_items
            iacc_v[...] = new_iacc
            item_b[2] = new_items.astype(bf16)
            items_on.start()
        else:
            grad_out[...] = item_grad.astype(bf16)
            grads_back.start()

        for node in reversed(range(len(NODES))):
            below = children_of(node)
            if not below:
                continue
            total = parts[block(node), :]
            for child in below:
                up(s, child).wait_recv()
                total = total + decode(income[s, block(child), :])
            if node > 0:
                outgo[s, block(node), :] = encode(total)
                up(s, node).start()
        if s == 0:
            loads[5].wait()
        new_users, new_uacc = adagrad(user_v[...], uacc_v[...], total + 0.1 * user_v[...])
        if s == 0:
            user_v[...] = new_users
            uacc_v[...] = new_uacc
            gather[1, block(0), :] = new_users.astype(bf16)
        else:
            users_o[...] = new_users

    grads_back.wait_recv()
    new_items, _ = adagrad(
        item_v[...], iacc_v[...], grad_in[...].astype(f32) + 0.1 * item_v[...]
    )
    items_o[...] = new_items

    items_on.wait_send()
    grads_back.wait_send()
    for s in range(strata):
        for node in range(1, len(NODES)):
            down(s, NODES[node][2], node).wait_send()
            up(s, node).wait_send()


def solution(mesh):
    n_user = mesh.shape["user"]
    count = len(NODES)

    def body(users, user_accum, items, item_accum, ratings, tile_mask):
        f32, bf16 = jnp.float32, jnp.bfloat16
        tile_mask = jnp.swapaxes(tile_mask, 1, 2)
        rows, rank = users.shape
        cols = items.shape[0]
        whole = count * rows
        sems = pltpu.SemaphoreType.DMA((2, count))
        return pl.pallas_call(
            functools.partial(kernel, n_user),
            out_shape=(
                jax.ShapeDtypeStruct((rows, rank), f32),
                jax.ShapeDtypeStruct((cols, rank), f32),
            ),
            in_specs=[pl.BlockSpec(memory_space=pl.ANY)] * 6,
            out_specs=(pl.BlockSpec(memory_space=pltpu.VMEM),) * 2,
            scratch_shapes=[
                pltpu.VMEM((2, whole, cols), jnp.int32),
                pltpu.SMEM(tile_mask.shape, jnp.int32),
                pltpu.VMEM((rows, rank), f32),
                pltpu.VMEM((rows, rank), f32),
                pltpu.VMEM((cols, rank), f32),
                pltpu.VMEM((cols, rank), f32),
                pltpu.VMEM((3, cols, rank), bf16),
                pltpu.VMEM((2, whole, rank), bf16),
                pltpu.VMEM((whole, cols), bf16),
                pltpu.VMEM((whole, rank), f32),
                pltpu.VMEM((2, whole, rank), jnp.int16),
                pltpu.VMEM((2, whole, rank), jnp.int16),
                pltpu.VMEM((cols, rank), bf16),
                pltpu.VMEM((cols, rank), bf16),
                pltpu.SemaphoreType.DMA((7,)),
                sems,
                sems,
                sems,
                sems,
                pltpu.SemaphoreType.DMA((2,)),
                pltpu.SemaphoreType.DMA((2,)),
            ],
            compiler_params=pltpu.CompilerParams(
                collective_id=0, has_side_effects=True, vmem_limit_bytes=56 * 2**20
            ),
        )(users, user_accum, items, item_accum, ratings, tile_mask)

    return jax.shard_map(
        body,
        mesh=mesh,
        in_specs=(
            P(("user", "item"), None),
            P(("user", "item"), None),
            P(("user", "item"), None),
            P(("user", "item"), None),
            P(None, "user", "item"),
            P(None, "user", "item"),
        ),
        out_specs=(P(("user", "item"), None), P(("user", "item"), None)),
        check_vma=False,
    )
```

```python
import functools
import math

import jax
import jax.numpy as jnp
from jax import lax
from jax.experimental import pallas as pl
from jax.experimental.pallas import tpu as pltpu
from jax.sharding import PartitionSpec as P

MESH = pl.DeviceIdType.MESH
RING = 8
OFFSETS = (0, 1, -1, 2, -2, 3, -3, 4)
GROUPS = ((0, 3), (3, 5), (5, 8))
SENDS = (7, 6, 5, 4, 3, 2, 1)

FLOOR, TOP = 1 / 16, 8192.0
STEPS = 32767 / math.log(1 + TOP / FLOOR)


def encode(x):
    steps = jnp.minimum(STEPS * jnp.log(1.0 + jnp.abs(x) * (1 / FLOOR)) + 0.5, 32767.0)
    return jnp.where(x < 0, -steps, steps).astype(jnp.int32).astype(jnp.int16)


def decode(code):
    steps = code.astype(jnp.int32).astype(jnp.float32)
    size = FLOOR * jnp.exp(jnp.abs(steps) * (1 / STEPS)) - FLOOR
    return jnp.where(steps < 0, -size, size)


def adagrad(param, accum, grad):
    accum = accum + grad * grad
    return param - 0.25 * grad / (jnp.sqrt(accum) + 1e-06), accum


def kernel(
    n_user, users_h, uacc_h, items_h, iacc_h, rates_h, mask_h, users_o, items_o,
    rates, rates_p, rates_out, rates_in, mask, mask_v, mask_p, user_v, uacc_v, item_v, iacc_v,
    item_b, item_new, gather, errors, part, outgo, income, grad_out, grad_in,
    load_sem, gs_send, gs_recv, rs_send, rs_recv, y_send, y_recv, it_send, it_recv,
):
    f32, bf16 = jnp.float32, jnp.bfloat16
    strata = rates_h.shape[0]
    rows, cols = users_h.shape[0], items_h.shape[0]
    plane = RING * rows
    tile_rows = 2 * plane // mask_h.shape[2]
    tile_cols = cols // mask_h.shape[1]
    u, i = lax.axis_index("user"), lax.axis_index("item")
    y, z = i // RING, i % RING
    across = (1 - y) * RING + z
    after, before = (u + 1) % n_user, (u + n_user - 1) % n_user

    def forth(k):
        return (u, y * RING + (z + OFFSETS[k] + RING) % RING)

    def place(k):
        return (z - OFFSETS[k] + RING) % RING

    def back(k):
        return (u, y * RING + place(k))

    def slot(k):
        return pl.ds(k * rows, rows)

    def half(s, p):
        return rates_h.at[s, pl.ds(pl.multiple_of(p * plane, plane), plane)]

    loads = [
        (users_h, user_v), (half(0, 1 - y), rates_p.at[0]), (items_h, item_v), (mask_h, mask.at[pl.ds(0, strata)]), (mask_h, mask_v),
        (half(0, y), rates.at[0]), (half(1, 1 - y), rates_p.at[1]), (iacc_h, iacc_v), (uacc_h, uacc_v),
        (half(1, y), rates.at[1]),
    ]
    loads = [pltpu.make_async_copy(src, dst, load_sem.at[k]) for k, (src, dst) in enumerate(loads)]
    for load in loads:
        load.start()

    near = [forth(k) for k in range(1, RING)] + [(v, j) for v in (after, before) for j in (i, across)] + [(u, across)]
    barrier = pltpu.get_barrier_semaphore()
    for there in near:
        pl.semaphore_signal(barrier, inc=1, device_id=there, device_id_type=MESH)

    def copy(src, dst, send, recv, there):
        return pltpu.make_async_remote_copy(
            src_ref=src, dst_ref=dst, send_sem=send, recv_sem=recv, device_id=there, device_id_type=MESH
        )

    def spread(s, k):
        return copy(gather.at[s, slot(0)], gather.at[s, slot(k)], gs_send.at[s, k], gs_recv.at[s, k], forth(k))

    def collect(s, k):
        return copy(outgo.at[s, slot(k)], income.at[s, slot(k)], rs_send.at[s, k], rs_recv.at[s, k], back(k))

    def to_partner(k, src, dst):
        return copy(src, dst, y_send.at[k], y_recv.at[k], (u, across))

    swap_items = to_partner(0, item_b.at[0, pl.ds(0, cols)], item_b.at[0, pl.ds(cols, cols)])
    swap_mask = to_partner(1, mask_v, mask_p)
    swap_grad = to_partner(2, grad_out.at[2], grad_in.at[2])
    swap_late = to_partner(3, rates_out.at[1], rates_in.at[1])
    swap_rates = []
    for n, (first, last) in enumerate(GROUPS):
        span = pl.ds(first * rows, (last - first) * rows)
        swap_rates.append(to_partner(4 + n, rates_out.at[0, span], rates_in.at[0, span]))
    items_on = [
        copy(item_new, item_b.at[1, pl.ds(n * cols, cols)], it_send.at[n], it_recv.at[n], (after, j))
        for n, j in enumerate((i, across))
    ]
    grads_back = [
        copy(grad_out.at[n], grad_in.at[n], it_send.at[2 + n], it_recv.at[2 + n], (before, j))
        for n, j in enumerate((i, across))
    ]

    def pack_rates(s):
        for k in range(RING):
            at = pl.ds(pl.multiple_of(place(k) * rows, rows), rows)
            rates_out[s, slot(k), :] = rates_p[s, at, :].astype(f32).astype(bf16)

    def compute(s, first, last):
        span = slice(first * rows, last * rows)
        item_rows = item_b[s]
        logits = lax.dot_general(
            gather[s, span, :], item_rows, (((1,), (1,)), ((), ())), preferred_element_type=f32
        )
        likely = 0.5 * jnp.tanh(0.5 * logits) + 0.5
        for k in range(first, last):
            at = pl.ds(pl.multiple_of(place(k) * rows, rows), rows)
            tile = (y * plane + place(k) * rows) // tile_rows
            mine = likely[(k - first) * rows : (k - first + 1) * rows]
            for h in range(2):
                rate = rates[s, at, :].astype(f32) if h == 0 else rates_in[s, slot(k), :].astype(f32)
                base = s + h * strata
                wrong = mine[:, h * cols : (h + 1) * cols] - rate
                for t in range(cols // tile_cols):
                    weight = mask[base, t, tile].astype(f32)
                    c = h * cols + t * tile_cols
                    errors[slot(k), c : c + tile_cols] = (
                        weight * wrong[:, t * tile_cols : (t + 1) * tile_cols]
                    ).astype(bf16)
        share = jnp.dot(errors[span, :], item_rows, preferred_element_type=f32)
        for k in range(first, last):
            mine = share[(k - first) * rows : (k - first + 1) * rows]
            if k > 0:
                outgo[s, slot(k), :] = encode(mine)
                collect(s, k).start()
            else:
                part[...] = mine

    def item_sum(s, h):
        return lax.dot_general(
            errors[:, h * cols : (h + 1) * cols], gather[s], (((0,), (0,)), ((), ())), preferred_element_type=f32
        )

    mask_s = mask.at[pl.ds(strata, strata)]
    loads[0].wait()
    gather[0, slot(0), :] = user_v[...].astype(bf16)
    loads[2].wait()
    item_b[0, pl.ds(0, cols), :] = item_v[...].astype(bf16)
    loads[1].wait()
    pack_rates(0)
    loads[4].wait()
    pl.semaphore_wait(barrier, len(near))

    for s in range(strata):
        for k in SENDS:
            spread(s, k).start()
        if s == 0:
            swap_items.start()
            swap_mask.start()
            for swap in swap_rates:
                swap.start()
            loads[6].wait()
            pack_rates(1)
            loads[3].wait()
            loads[5].wait()
            swap_mask.wait_recv()
            local = pltpu.make_async_copy(mask_p, mask_s, load_sem.at[10])
            local.start()
            local.wait()
            swap_items.wait_recv()
        else:
            loads[9].wait()
            swap_late.wait_recv()
            for on in items_on:
                on.wait_recv()
        for n, (first, last) in enumerate(GROUPS):
            for k in range(max(first, 1), last):
                spread(s, k).wait_recv()
            if s == 0:
                swap_rates[n].wait_recv()
            compute(s, first, last)

        if s == 0:
            grad_out[2] = item_sum(s, 1).astype(bf16)
            swap_grad.start()
            swap_late.start()
            item_grad = item_sum(s, 0)
            loads[7].wait()
            swap_grad.wait_recv()
            item_grad = item_grad + grad_in[2].astype(f32) + 0.1 * item_v[...]
            new_items, new_iacc = adagrad(item_v[...], iacc_v[...], item_grad)
            item_v[...] = new_items
            iacc_v[...] = new_iacc
            item_new[...] = new_items.astype(bf16)
            for on in items_on:
                on.start()
        else:
            for n in range(2):
                grad_out[n] = item_sum(s, n).astype(bf16)
                grads_back[n].start()

        total = part[...] + 0.1 * user_v[...]
        for k in range(1, RING):
            collect(s, k).wait_recv()
            total = total + decode(income[s, slot(k), :])
        if s == 0:
            loads[8].wait()
        new_users, new_uacc = adagrad(user_v[...], uacc_v[...], total)
        if s == 0:
            user_v[...] = new_users
            uacc_v[...] = new_uacc
            gather[1, slot(0), :] = new_users.astype(bf16)
        else:
            users_o[...] = new_users

    for grads in grads_back:
        grads.wait_recv()
    item_grad = grad_in[0].astype(f32) + grad_in[1].astype(f32) + 0.1 * item_v[...]
    new_items, _ = adagrad(item_v[...], iacc_v[...], item_grad)
    items_o[...] = new_items

    for sent in [swap_items, swap_mask, swap_grad, swap_late, *swap_rates, *items_on, *grads_back]:
        sent.wait_send()
    for s in range(strata):
        for k in range(1, RING):
            spread(s, k).wait_send()
            collect(s, k).wait_send()


def solution(mesh):
    n_user = mesh.shape["user"]

    def body(users, user_accum, items, item_accum, ratings, tile_mask):
        f32, bf16, i32 = jnp.float32, jnp.bfloat16, jnp.int32
        tile_mask = jnp.swapaxes(tile_mask, 1, 2)
        strata = ratings.shape[0]
        rows, rank = users.shape
        cols = items.shape[0]
        plane = RING * rows
        ring_sems = pltpu.SemaphoreType.DMA((strata, RING))
        return pl.pallas_call(
            functools.partial(kernel, n_user),
            out_shape=(
                jax.ShapeDtypeStruct((rows, rank), f32),
                jax.ShapeDtypeStruct((cols, rank), f32),
            ),
            in_specs=[pl.BlockSpec(memory_space=pl.ANY)] * 6,
            out_specs=(pl.BlockSpec(memory_space=pltpu.VMEM),) * 2,
            scratch_shapes=[
                pltpu.VMEM((strata, plane, cols), i32),
                pltpu.VMEM((strata, plane, cols), i32),
                pltpu.VMEM((strata, plane, cols), bf16),
                pltpu.VMEM((strata, plane, cols), bf16),
                pltpu.SMEM((2 * strata, *tile_mask.shape[1:]), i32),
                pltpu.VMEM(tile_mask.shape, i32),
                pltpu.VMEM(tile_mask.shape, i32),
                pltpu.VMEM((rows, rank), f32),
                pltpu.VMEM((rows, rank), f32),
                pltpu.VMEM((cols, rank), f32),
                pltpu.VMEM((cols, rank), f32),
                pltpu.VMEM((strata, 2 * cols, rank), bf16),
                pltpu.VMEM((cols, rank), bf16),
                pltpu.VMEM((strata, plane, rank), bf16),
                pltpu.VMEM((plane, 2 * cols), bf16),
                pltpu.VMEM((rows, rank), f32),
                pltpu.VMEM((strata, plane, rank), jnp.int16),
                pltpu.VMEM((strata, plane, rank), jnp.int16),
                pltpu.VMEM((3, cols, rank), bf16),
                pltpu.VMEM((3, cols, rank), bf16),
                pltpu.SemaphoreType.DMA((11,)),
                ring_sems,
                ring_sems,
                ring_sems,
                ring_sems,
                pltpu.SemaphoreType.DMA((4 + len(GROUPS),)),
                pltpu.SemaphoreType.DMA((4 + len(GROUPS),)),
                pltpu.SemaphoreType.DMA((4,)),
                pltpu.SemaphoreType.DMA((4,)),
            ],
            compiler_params=pltpu.CompilerParams(
                collective_id=0, has_side_effects=True, vmem_limit_bytes=56 * 2**20
            ),
        )(users, user_accum, items, item_accum, ratings, tile_mask)

    return jax.shard_map(
        body,
        mesh=mesh,
        in_specs=(
            P(("user", "item"), None),
            P(("user", "item"), None),
            P(("user", "item"), None),
            P(("user", "item"), None),
            P(None, "user", "item"),
            P(None, "user", "item"),
        ),
        out_specs=(P(("user", "item"), None), P(("user", "item"), None)),
        check_vma=False,
    )
```

```python
import functools
import math

import jax
import jax.numpy as jnp
from jax import lax
from jax.experimental import pallas as pl
from jax.experimental.pallas import tpu as pltpu
from jax.sharding import PartitionSpec as P

MESH = pl.DeviceIdType.MESH
RING = 8
OFFSETS = (0, 4, 3, -3, 2, -2, 1, -1)
GROUPS = ((0, 2), (2, 4), (4, 6), (6, 8))
SHARES = ((0, 4), (4, 8))
SENDS = (1, 2, 3, 4, 5, 6, 7)

FLOOR, TOP = 1 / 16, 8192.0
STEPS = 32767 / math.log(1 + TOP / FLOOR)


def encode(x):
    steps = jnp.minimum(STEPS * jnp.log(1.0 + jnp.abs(x) * (1 / FLOOR)) + 0.5, 32767.0)
    return jnp.where(x < 0, -steps, steps).astype(jnp.int32).astype(jnp.int16)


def decode(code):
    steps = code.astype(jnp.int32).astype(jnp.float32)
    size = FLOOR * jnp.exp(jnp.abs(steps) * (1 / STEPS)) - FLOOR
    return jnp.where(steps < 0, -size, size)


def adagrad(param, accum, grad):
    accum = accum + grad * grad
    return param - 0.25 * grad / (jnp.sqrt(accum) + 1e-06), accum


def kernel(
    n_user, users_h, uacc_h, items_h, iacc_h, rates_h, mask_h, users_o, items_o,
    rates, rates_p, rates_out, rates_in, mask, mask_v, mask_p, user_v, uacc_v, item_v, iacc_v,
    item_b, item_new, item_grad, gather, errors, part, outgo, income, grad_out, grad_in,
    load_sem, gs_send, gs_recv, rs_send, rs_recv, y_send, y_recv, it_send, it_recv,
):
    f32, bf16 = jnp.float32, jnp.bfloat16
    strata = rates_h.shape[0]
    rows, cols = users_h.shape[0], items_h.shape[0]
    plane = RING * rows
    tile_rows = 2 * plane // mask_h.shape[2]
    tile_cols = cols // mask_h.shape[1]
    u, i = lax.axis_index("user"), lax.axis_index("item")
    y, z = i // RING, i % RING
    across = (1 - y) * RING + z
    after, before = (u + 1) % n_user, (u + n_user - 1) % n_user

    def forth(k):
        return (u, y * RING + (z + OFFSETS[k] + RING) % RING)

    def place(k):
        return (z - OFFSETS[k] + RING) % RING

    def back(k):
        return (u, y * RING + place(k))

    def slot(k):
        return pl.ds(k * rows, rows)

    def half(s, p):
        return rates_h.at[s, pl.ds(pl.multiple_of(p * plane, plane), plane)]

    loads = [
        (users_h, user_v), (half(0, 1 - y), rates_p.at[0]), (items_h, item_v), (mask_h, mask.at[pl.ds(0, strata)]), (mask_h, mask_v),
        (half(0, y), rates.at[0]), (half(1, 1 - y), rates_p.at[1]), (iacc_h, iacc_v), (uacc_h, uacc_v),
        (half(1, y), rates.at[1]),
    ]
    loads = [pltpu.make_async_copy(src, dst, load_sem.at[k]) for k, (src, dst) in enumerate(loads)]
    for load in loads:
        load.start()

    near = [forth(k) for k in range(1, RING)] + [(v, j) for v in (after, before) for j in (i, across)] + [(u, across)]
    barrier = pltpu.get_barrier_semaphore()
    for there in near:
        pl.semaphore_signal(barrier, inc=1, device_id=there, device_id_type=MESH)

    def copy(src, dst, send, recv, there):
        return pltpu.make_async_remote_copy(
            src_ref=src, dst_ref=dst, send_sem=send, recv_sem=recv, device_id=there, device_id_type=MESH
        )

    def spread(s, k):
        return copy(gather.at[s, slot(0)], gather.at[s, slot(k)], gs_send.at[s, k], gs_recv.at[s, k], forth(k))

    def collect(s, k):
        return copy(outgo.at[s, slot(k)], income.at[s, slot(k)], rs_send.at[s, k], rs_recv.at[s, k], back(k))

    def to_partner(k, src, dst):
        return copy(src, dst, y_send.at[k], y_recv.at[k], (u, across))

    swap_items = to_partner(0, item_b.at[0, pl.ds(0, cols)], item_b.at[0, pl.ds(cols, cols)])
    swap_mask = to_partner(1, mask_v, mask_p)
    swap_grad = to_partner(2, grad_out.at[2], grad_in.at[2])
    swap_late = to_partner(3, rates_out.at[1], rates_in.at[1])
    swap_rates = []
    for n, (first, last) in enumerate(GROUPS):
        span = pl.ds(first * rows, (last - first) * rows)
        swap_rates.append(to_partner(4 + n, rates_out.at[0, span], rates_in.at[0, span]))
    items_on = [
        copy(item_new, item_b.at[1, pl.ds(n * cols, cols)], it_send.at[n], it_recv.at[n], (after, j))
        for n, j in enumerate((i, across))
    ]
    grads_back = [
        copy(grad_out.at[n], grad_in.at[n], it_send.at[2 + n], it_recv.at[2 + n], (before, j))
        for n, j in enumerate((i, across))
    ]

    def pack_rates(s):
        for k in range(RING):
            at = pl.ds(pl.multiple_of(place(k) * rows, rows), rows)
            rates_out[s, slot(k), :] = rates_p[s, at, :].astype(f32).astype(bf16)

    def compute(s, h, first, last):
        span = slice(first * rows, last * rows)
        logits = lax.dot_general(
            gather[s, span, :], item_b[s, h * cols : (h + 1) * cols, :], (((1,), (1,)), ((), ())),
            preferred_element_type=f32,
        )
        likely = 0.5 * jnp.tanh(0.5 * logits) + 0.5
        for k in range(first, last):
            at = pl.ds(pl.multiple_of(place(k) * rows, rows), rows)
            tile = (y * plane + place(k) * rows) // tile_rows
            rate = rates[s, at, :].astype(f32) if h == 0 else rates_in[s, slot(k), :].astype(f32)
            wrong = likely[(k - first) * rows : (k - first + 1) * rows] - rate
            for t in range(cols // tile_cols):
                weight = mask[s + h * strata, t, tile].astype(f32)
                c = slice(t * tile_cols, (t + 1) * tile_cols)
                errors[slot(k), h * cols + t * tile_cols : h * cols + (t + 1) * tile_cols] = (
                    weight * wrong[:, c]
                ).astype(bf16)

    def share_out(s, first, last):
        span = slice(first * rows, last * rows)
        share = jnp.dot(errors[span, :], item_b[s], preferred_element_type=f32)
        for k in range(first, last):
            mine = share[(k - first) * rows : (k - first + 1) * rows]
            if k > 0:
                outgo[s, slot(k), :] = encode(mine)
                collect(s, k).start()
            else:
                part[...] = mine

    def item_sum(s, h):
        return lax.dot_general(
            errors[:, h * cols : (h + 1) * cols], gather[s], (((0,), (0,)), ((), ())), preferred_element_type=f32
        )

    mask_s = mask.at[pl.ds(strata, strata)]
    loads[0].wait()
    gather[0, slot(0), :] = user_v[...].astype(bf16)
    loads[2].wait()
    item_b[0, pl.ds(0, cols), :] = item_v[...].astype(bf16)
    loads[1].wait()
    pack_rates(0)
    loads[4].wait()
    pl.semaphore_wait(barrier, len(near))

    for s in range(strata):
        for k in SENDS:
            spread(s, k).start()
        if s == 0:
            swap_mask.start()
            swap_items.start()
            for swap in swap_rates:
                swap.start()
            loads[6].wait()
            pack_rates(1)
            loads[3].wait()
            loads[5].wait()
        else:
            loads[9].wait()
            items_on[0].wait_recv()
        for first, last in GROUPS:
            for k in range(max(first, 1), last):
                spread(s, k).wait_recv()
            compute(s, 0, first, last)
        if s == 0:
            item_grad[...] = item_sum(s, 0)
            swap_mask.wait_recv()
            local = pltpu.make_async_copy(mask_p, mask_s, load_sem.at[10])
            local.start()
            local.wait()
            swap_items.wait_recv()
        else:
            grad_out[0] = item_sum(s, 0).astype(bf16)
            grads_back[0].start()
            swap_late.wait_recv()
            items_on[1].wait_recv()
        for n, (first, last) in enumerate(GROUPS):
            if s == 0:
                swap_rates[n].wait_recv()
            compute(s, 1, first, last)
            if s == 0:
                share_out(s, first, last)
        if s == 0:
            grad_out[2] = item_sum(s, 1).astype(bf16)
            swap_grad.start()
            swap_late.start()
        else:
            grad_out[1] = item_sum(s, 1).astype(bf16)
            grads_back[1].start()
        if s > 0:
            for first, last in SHARES:
                share_out(s, first, last)

        if s == 0:
            loads[7].wait()
            swap_grad.wait_recv()
            whole = item_grad[...] + grad_in[2].astype(f32) + 0.1 * item_v[...]
            new_items, new_iacc = adagrad(item_v[...], iacc_v[...], whole)
            item_v[...] = new_items
            iacc_v[...] = new_iacc
            item_new[...] = new_items.astype(bf16)
            for on in items_on:
                on.start()

        total = part[...] + 0.1 * user_v[...]
        for k in range(1, RING):
            collect(s, k).wait_recv()
            total = total + decode(income[s, slot(k), :])
        if s == 0:
            loads[8].wait()
        new_users, new_uacc = adagrad(user_v[...], uacc_v[...], total)
        if s == 0:
            user_v[...] = new_users
            uacc_v[...] = new_uacc
            gather[1, slot(0), :] = new_users.astype(bf16)
        else:
            users_o[...] = new_users

    for grads in grads_back:
        grads.wait_recv()
    whole = grad_in[0].astype(f32) + grad_in[1].astype(f32) + 0.1 * item_v[...]
    new_items, _ = adagrad(item_v[...], iacc_v[...], whole)
    items_o[...] = new_items

    for sent in [swap_items, swap_mask, swap_grad, swap_late, *swap_rates, *items_on, *grads_back]:
        sent.wait_send()
    for s in range(strata):
        for k in range(1, RING):
            spread(s, k).wait_send()
            collect(s, k).wait_send()


def hand_over(users_i, items_i, users_o, items_o):
    users_o[...] = users_i[...]
    items_o[...] = items_i[...]


def solution(mesh):
    n_user = mesh.shape["user"]

    def body(users, user_accum, items, item_accum, ratings, tile_mask):
        f32, bf16, i32 = jnp.float32, jnp.bfloat16, jnp.int32
        tile_mask = jnp.swapaxes(tile_mask, 1, 2)
        strata = ratings.shape[0]
        rows, rank = users.shape
        cols = items.shape[0]
        plane = RING * rows
        ring_sems = pltpu.SemaphoreType.DMA((strata, RING))
        results = pl.pallas_call(
            functools.partial(kernel, n_user),
            out_shape=(
                jax.ShapeDtypeStruct((rows, rank), f32),
                jax.ShapeDtypeStruct((cols, rank), f32),
            ),
            in_specs=[pl.BlockSpec(memory_space=pl.ANY)] * 6,
            out_specs=(pl.BlockSpec(memory_space=pltpu.VMEM),) * 2,
            scratch_shapes=[
                pltpu.VMEM((strata, plane, cols), i32),
                pltpu.VMEM((strata, plane, cols), i32),
                pltpu.VMEM((strata, plane, cols), bf16),
                pltpu.VMEM((strata, plane, cols), bf16),
                pltpu.SMEM((2 * strata, *tile_mask.shape[1:]), i32),
                pltpu.VMEM(tile_mask.shape, i32),
                pltpu.VMEM(tile_mask.shape, i32),
                pltpu.VMEM((rows, rank), f32),
                pltpu.VMEM((rows, rank), f32),
                pltpu.VMEM((cols, rank), f32),
                pltpu.VMEM((cols, rank), f32),
                pltpu.VMEM((strata, 2 * cols, rank), bf16),
                pltpu.VMEM((cols, rank), bf16),
                pltpu.VMEM((cols, rank), f32),
                pltpu.VMEM((strata, plane, rank), bf16),
                pltpu.VMEM((plane, 2 * cols), bf16),
                pltpu.VMEM((rows, rank), f32),
                pltpu.VMEM((strata, plane, rank), jnp.int16),
                pltpu.VMEM((strata, plane, rank), jnp.int16),
                pltpu.VMEM((3, cols, rank), bf16),
                pltpu.VMEM((3, cols, rank), bf16),
                pltpu.SemaphoreType.DMA((11,)),
                ring_sems,
                ring_sems,
                ring_sems,
                ring_sems,
                pltpu.SemaphoreType.DMA((4 + len(GROUPS),)),
                pltpu.SemaphoreType.DMA((4 + len(GROUPS),)),
                pltpu.SemaphoreType.DMA((4,)),
                pltpu.SemaphoreType.DMA((4,)),
            ],
            compiler_params=pltpu.CompilerParams(
                collective_id=0, has_side_effects=True, vmem_limit_bytes=56 * 2**20
            ),
        )(users, user_accum, items, item_accum, ratings, tile_mask)
        return pl.pallas_call(
            hand_over,
            out_shape=tuple(jax.ShapeDtypeStruct(r.shape, r.dtype) for r in results),
        )(*results)

    return jax.shard_map(
        body,
        mesh=mesh,
        in_specs=(
            P(("user", "item"), None),
            P(("user", "item"), None),
            P(("user", "item"), None),
            P(("user", "item"), None),
            P(None, "user", "item"),
            P(None, "user", "item"),
        ),
        out_specs=(P(("user", "item"), None), P(("user", "item"), None)),
        check_vma=False,
    )
```

```python
import functools
import math

import jax
import jax.numpy as jnp
from jax import lax
from jax.experimental import pallas as pl
from jax.experimental.pallas import tpu as pltpu
from jax.sharding import PartitionSpec as P

MESH = pl.DeviceIdType.MESH
RING = 8
OFFSETS = (0, 4, 3, -3, 2, -2, 1, -1)
GROUPS = ((0, 2), (2, 4), (4, 6), (6, 8))
SHARES = ((0, 4), (4, 8))
SENDS = (1, 2, 3, 4, 5, 6, 7)

FLOOR, TOP = 1 / 16, 8192.0
STEPS = 32767 / math.log(1 + TOP / FLOOR)


def encode(x):
    steps = jnp.minimum(STEPS * jnp.log(1.0 + jnp.abs(x) * (1 / FLOOR)) + 0.5, 32767.0)
    return jnp.where(x < 0, -steps, steps).astype(jnp.int32).astype(jnp.int16)


def decode(code):
    steps = code.astype(jnp.int32).astype(jnp.float32)
    size = FLOOR * jnp.exp(jnp.abs(steps) * (1 / STEPS)) - FLOOR
    return jnp.where(steps < 0, -size, size)


def adagrad(param, accum, grad):
    accum = accum + grad * grad
    return param - 0.25 * grad / (jnp.sqrt(accum) + 1e-06), accum


def kernel(
    n_user, users_h, uacc_h, items_h, iacc_h, rates_h, mask_h, users_o, items_o,
    rates, rates_p, rates_out, rates_in, mask, mask_v, mask_p, user_v, uacc_v, item_v, iacc_v,
    item_b, item_new, item_grad, gather, errors, part, outgo, income, grad_out, grad_in,
    load_sem, gs_send, gs_recv, rs_send, rs_recv, y_send, y_recv, it_send, it_recv,
):
    f32, bf16 = jnp.float32, jnp.bfloat16
    strata = rates_h.shape[0]
    rows, cols = users_h.shape[0], items_h.shape[0]
    plane = RING * rows
    tile_rows = 2 * plane // mask_h.shape[2]
    tile_cols = cols // mask_h.shape[1]
    u, i = lax.axis_index("user"), lax.axis_index("item")
    y, z = i // RING, i % RING
    across = (1 - y) * RING + z
    after, before = (u + 1) % n_user, (u + n_user - 1) % n_user

    def forth(k):
        return (u, y * RING + (z + OFFSETS[k] + RING) % RING)

    def place(k):
        return (z - OFFSETS[k] + RING) % RING

    def back(k):
        return (u, y * RING + place(k))

    def slot(k):
        return pl.ds(k * rows, rows)

    def half(s, p):
        return rates_h.at[s, pl.ds(pl.multiple_of(p * plane, plane), plane)]

    loads = [
        (users_h, user_v), (half(0, 1 - y), rates_p.at[0]), (items_h, item_v), (mask_h, mask.at[pl.ds(0, strata)]), (mask_h, mask_v),
        (half(0, y), rates.at[0]), (half(1, 1 - y), rates_p.at[1]), (iacc_h, iacc_v), (uacc_h, uacc_v),
        (half(1, y), rates.at[1]),
    ]
    loads = [pltpu.make_async_copy(src, dst, load_sem.at[k]) for k, (src, dst) in enumerate(loads)]
    near = [forth(k) for k in range(1, RING)] + [(v, j) for v in (after, before) for j in (i, across)] + [(u, across)]
    barrier = pltpu.get_barrier_semaphore()
    for there in near:
        pl.semaphore_signal(barrier, inc=1, device_id=there, device_id_type=MESH)
    for k in (0, 2, 1, *range(3, len(loads))):
        loads[k].start()

    def copy(src, dst, send, recv, there):
        return pltpu.make_async_remote_copy(
            src_ref=src, dst_ref=dst, send_sem=send, recv_sem=recv, device_id=there, device_id_type=MESH
        )

    def spread(s, k):
        return copy(gather.at[s, slot(0)], gather.at[s, slot(k)], gs_send.at[s, k], gs_recv.at[s, k], forth(k))

    def collect(s, k):
        return copy(outgo.at[s, slot(k)], income.at[s, slot(k)], rs_send.at[s, k], rs_recv.at[s, k], back(k))

    def to_partner(k, src, dst):
        return copy(src, dst, y_send.at[k], y_recv.at[k], (u, across))

    swap_items = to_partner(0, item_b.at[0, pl.ds(0, cols)], item_b.at[0, pl.ds(cols, cols)])
    swap_mask = to_partner(1, mask_v, mask_p)
    swap_grad = to_partner(2, grad_out.at[2], grad_in.at[2])
    swap_late = to_partner(3, rates_out.at[1], rates_in.at[1])
    swap_rates = []
    for n, (first, last) in enumerate(GROUPS):
        span = pl.ds(first * rows, (last - first) * rows)
        swap_rates.append(to_partner(4 + n, rates_out.at[0, span], rates_in.at[0, span]))
    items_on = [
        copy(item_new, item_b.at[1, pl.ds(n * cols, cols)], it_send.at[n], it_recv.at[n], (after, j))
        for n, j in enumerate((i, across))
    ]
    grads_back = [
        copy(grad_out.at[n], grad_in.at[n], it_send.at[2 + n], it_recv.at[2 + n], (before, j))
        for n, j in enumerate((i, across))
    ]

    def pack_rates(s):
        for k in range(RING):
            at = pl.ds(pl.multiple_of(place(k) * rows, rows), rows)
            rates_out[s, slot(k), :] = rates_p[s, at, :].astype(f32).astype(bf16)

    def compute(s, h, first, last):
        span = slice(first * rows, last * rows)
        logits = lax.dot_general(
            gather[s, span, :], item_b[s, h * cols : (h + 1) * cols, :], (((1,), (1,)), ((), ())),
            preferred_element_type=f32,
        )
        likely = 0.5 * jnp.tanh(0.5 * logits) + 0.5
        for k in range(first, last):
            at = pl.ds(pl.multiple_of(place(k) * rows, rows), rows)
            tile = (y * plane + place(k) * rows) // tile_rows
            rate = rates[s, at, :].astype(f32) if h == 0 else rates_in[s, slot(k), :].astype(f32)
            wrong = likely[(k - first) * rows : (k - first + 1) * rows] - rate
            for t in range(cols // tile_cols):
                weight = mask[s + h * strata, t, tile].astype(f32)
                c = slice(t * tile_cols, (t + 1) * tile_cols)
                errors[slot(k), h * cols + t * tile_cols : h * cols + (t + 1) * tile_cols] = (
                    weight * wrong[:, c]
                ).astype(bf16)

    def share_out(s, first, last):
        span = slice(first * rows, last * rows)
        share = jnp.dot(errors[span, :], item_b[s], preferred_element_type=f32)
        for k in range(first, last):
            mine = share[(k - first) * rows : (k - first + 1) * rows]
            if k > 0:
                outgo[s, slot(k), :] = encode(mine)
                collect(s, k).start()
            else:
                part[...] = mine

    def item_sum(s, h):
        return lax.dot_general(
            errors[:, h * cols : (h + 1) * cols], gather[s], (((0,), (0,)), ((), ())), preferred_element_type=f32
        )

    mask_s = mask.at[pl.ds(strata, strata)]
    loads[0].wait()
    gather[0, slot(0), :] = user_v[...].astype(bf16)
    loads[2].wait()
    item_b[0, pl.ds(0, cols), :] = item_v[...].astype(bf16)
    pl.semaphore_wait(barrier, len(near))

    for s in range(strata):
        for k in SENDS:
            spread(s, k).start()
        if s == 0:
            swap_items.start()
            loads[4].wait()
            swap_mask.start()
            loads[1].wait()
            pack_rates(0)
            for swap in swap_rates:
                swap.start()
            loads[6].wait()
            pack_rates(1)
            loads[3].wait()
            loads[5].wait()
        else:
            loads[9].wait()
            items_on[0].wait_recv()
        for first, last in GROUPS:
            for k in range(max(first, 1), last):
                spread(s, k).wait_recv()
            compute(s, 0, first, last)
        if s == 0:
            item_grad[...] = item_sum(s, 0)
            swap_mask.wait_recv()
            local = pltpu.make_async_copy(mask_p, mask_s, load_sem.at[10])
            local.start()
            local.wait()
            swap_items.wait_recv()
        else:
            grad_out[0] = item_sum(s, 0).astype(bf16)
            grads_back[0].start()
            swap_late.wait_recv()
            items_on[1].wait_recv()
        for n, (first, last) in enumerate(GROUPS):
            if s == 0:
                swap_rates[n].wait_recv()
            compute(s, 1, first, last)
            if s == 0:
                share_out(s, first, last)
        if s == 0:
            grad_out[2] = item_sum(s, 1).astype(bf16)
            swap_grad.start()
            swap_late.start()
        else:
            grad_out[1] = item_sum(s, 1).astype(bf16)
            grads_back[1].start()
        if s > 0:
            for first, last in SHARES:
                share_out(s, first, last)

        if s == 0:
            loads[7].wait()
            swap_grad.wait_recv()
            whole = item_grad[...] + grad_in[2].astype(f32) + 0.1 * item_v[...]
            new_items, new_iacc = adagrad(item_v[...], iacc_v[...], whole)
            item_v[...] = new_items
            iacc_v[...] = new_iacc
            item_new[...] = new_items.astype(bf16)
            for on in items_on:
                on.start()

        total = part[...] + 0.1 * user_v[...]
        for k in range(1, RING):
            collect(s, k).wait_recv()
            total = total + decode(income[s, slot(k), :])
        if s == 0:
            loads[8].wait()
        new_users, new_uacc = adagrad(user_v[...], uacc_v[...], total)
        if s == 0:
            user_v[...] = new_users
            uacc_v[...] = new_uacc
            gather[1, slot(0), :] = new_users.astype(bf16)
        else:
            users_o[...] = new_users

    for grads in grads_back:
        grads.wait_recv()
    whole = grad_in[0].astype(f32) + grad_in[1].astype(f32) + 0.1 * item_v[...]
    new_items, _ = adagrad(item_v[...], iacc_v[...], whole)
    items_o[...] = new_items

    for sent in [swap_items, swap_mask, swap_grad, swap_late, *swap_rates, *items_on, *grads_back]:
        sent.wait_send()
    for s in range(strata):
        for k in range(1, RING):
            spread(s, k).wait_send()
            collect(s, k).wait_send()


def hand_over(users_i, items_i, users_o, items_o):
    users_o[...] = users_i[...]
    items_o[...] = items_i[...]


def solution(mesh):
    n_user = mesh.shape["user"]

    def body(users, user_accum, items, item_accum, ratings, tile_mask):
        f32, bf16, i32 = jnp.float32, jnp.bfloat16, jnp.int32
        tile_mask = jnp.swapaxes(tile_mask, 1, 2)
        strata = ratings.shape[0]
        rows, rank = users.shape
        cols = items.shape[0]
        plane = RING * rows
        ring_sems = pltpu.SemaphoreType.DMA((strata, RING))
        results = pl.pallas_call(
            functools.partial(kernel, n_user),
            out_shape=(
                jax.ShapeDtypeStruct((rows, rank), f32),
                jax.ShapeDtypeStruct((cols, rank), f32),
            ),
            in_specs=[pl.BlockSpec(memory_space=pl.ANY)] * 6,
            out_specs=(pl.BlockSpec(memory_space=pltpu.VMEM),) * 2,
            scratch_shapes=[
                pltpu.VMEM((strata, plane, cols), i32),
                pltpu.VMEM((strata, plane, cols), i32),
                pltpu.VMEM((strata, plane, cols), bf16),
                pltpu.VMEM((strata, plane, cols), bf16),
                pltpu.SMEM((2 * strata, *tile_mask.shape[1:]), i32),
                pltpu.VMEM(tile_mask.shape, i32),
                pltpu.VMEM(tile_mask.shape, i32),
                pltpu.VMEM((rows, rank), f32),
                pltpu.VMEM((rows, rank), f32),
                pltpu.VMEM((cols, rank), f32),
                pltpu.VMEM((cols, rank), f32),
                pltpu.VMEM((strata, 2 * cols, rank), bf16),
                pltpu.VMEM((cols, rank), bf16),
                pltpu.VMEM((cols, rank), f32),
                pltpu.VMEM((strata, plane, rank), bf16),
                pltpu.VMEM((plane, 2 * cols), bf16),
                pltpu.VMEM((rows, rank), f32),
                pltpu.VMEM((strata, plane, rank), jnp.int16),
                pltpu.VMEM((strata, plane, rank), jnp.int16),
                pltpu.VMEM((3, cols, rank), bf16),
                pltpu.VMEM((3, cols, rank), bf16),
                pltpu.SemaphoreType.DMA((11,)),
                ring_sems,
                ring_sems,
                ring_sems,
                ring_sems,
                pltpu.SemaphoreType.DMA((4 + len(GROUPS),)),
                pltpu.SemaphoreType.DMA((4 + len(GROUPS),)),
                pltpu.SemaphoreType.DMA((4,)),
                pltpu.SemaphoreType.DMA((4,)),
            ],
            compiler_params=pltpu.CompilerParams(
                collective_id=0, has_side_effects=True, vmem_limit_bytes=56 * 2**20
            ),
        )(users, user_accum, items, item_accum, ratings, tile_mask)
        return pl.pallas_call(
            hand_over,
            out_shape=tuple(jax.ShapeDtypeStruct(r.shape, r.dtype) for r in results),
        )(*results)

    return jax.shard_map(
        body,
        mesh=mesh,
        in_specs=(
            P(("user", "item"), None),
            P(("user", "item"), None),
            P(("user", "item"), None),
            P(("user", "item"), None),
            P(None, "user", "item"),
            P(None, "user", "item"),
        ),
        out_specs=(P(("user", "item"), None), P(("user", "item"), None)),
        check_vma=False,
    )
```
